512 devices in a mesh: dp: 128 (over x, y, z_lo), grad: 4 (over z_hi, core).
Axes of the slice: x: 4, y: 4, z: 16 (z_hi: 2, z_lo: 8; z = z_hi * 8 + z_lo), core: 2. Of those that a mesh axis runs over, the one named last changes fastest.
Arguments:
- activations: bfloat16 [1024, 6144], P('grad', 'dp'), may hold values from -6 to 6
- output_grads: bfloat16 [1024, 6144], P('grad', 'dp'), may hold values from -0.1875 to 0.1875
- output_inverse: bfloat16 [6144, 3072], P('dp'), may hold values from -0.078125 to 0.078125
- input_inverse: bfloat16 [6144, 6144], P('dp'), may hold values from -0.078125 to 0.078125
- owner_table: int32 [128], replicated, may hold values from 0 to 127, each once
- factor_slab: float32 [6144, 6144], P('grad', 'dp'), may hold values from -6 to 6
- momentum: float32 [6144, 3072], P('dp', 'grad'), may hold values from -6 to 6
Outputs:
- new_momentum: float32 [6144, 3072], P('dp', 'grad')
- new_factor: float32 [6144, 6144], P('grad', 'dp')
The draws below stay inside these ranges and needn't reach their ends.
Inputs may be any that keep to these rules, and one draw needn't show every extreme that they name: owner_table is a permutation: every natural feature block is stored exactly once.
All inputs are finite; a program needn't handle non-finite values.
Results may differ from the reference program's by a relative error of at most 0.007.
Values may be sent and summed in bfloat16 or wider, within the bound.
A program may use at most 64 MiB of HBM per device.

```python
import jax
import jax.numpy as jnp

D = 6144
B = 6144
R = 3072
TOKENS = 1024
N_DP = 128


def steps_of(stream_key, shape, cuts, low, largest):
    gain = 1.0
    for dim, blocks in cuts:
        heights = jax.random.uniform(jax.random.fold_in(jax.random.fold_in(stream_key, 6), dim), (blocks,), jnp.float32, low / len(cuts), largest / len(cuts))
        gain = gain * jnp.repeat(jnp.exp(heights), shape[dim] // blocks).reshape((-1,) + (1,) * (len(shape) - 1 - dim))
    return gain


def gaussian(key, extent, width, bound, cuts=(), held_as=jnp.bfloat16):
    loudness = steps_of(key, extent, cuts, -0.22, 0.18) if cuts else 1.0
    array = jax.random.normal(key, extent, jnp.float32) * width * loudness
    return jnp.minimum(jnp.maximum(array, -bound), bound).astype(held_as)


def setup_inputs(seed: int = 0) -> dict:
    splits = jax.random.split(jax.random.key(seed), 8)
    activations = gaussian(splits[0], (TOKENS, D), 1.0, 6.0, ((0, 4), (1, 128)))
    output_grads = gaussian(splits[1], (TOKENS, B), TOKENS ** -0.5, 0.1875, ((0, 4), (1, 128)))
    output_inverse = gaussian(splits[2], (B, R), B ** -0.5, 0.078125, ((0, 128),))
    input_inverse = gaussian(splits[3], (D, D), D ** -0.5, 0.078125, ((0, 128),))
    owner_table = jax.random.permutation(splits[4], N_DP).astype(jnp.int32)
    factor_slab = gaussian(splits[5], (D, D), 1.0, 6.0, ((0, 4), (1, 128)), jnp.float32)
    momentum = gaussian(splits[6], (D, R), 1.0, 6.0, ((0, 128), (1, 4)), jnp.float32)
    return dict(activations=activations, output_grads=output_grads, output_inverse=output_inverse, input_inverse=input_inverse, owner_table=owner_table, factor_slab=factor_slab, momentum=momentum)


def reference(activations, output_grads, output_inverse, input_inverse, owner_table, factor_slab, momentum):
    projected = jnp.dot(output_grads, output_inverse, preferred_element_type=jnp.float32).astype(jnp.bfloat16)
    gradient = jnp.dot(activations.T, projected, preferred_element_type=jnp.float32).astype(jnp.bfloat16)
    covariance = jnp.dot(activations.T, activations, preferred_element_type=jnp.float32) / TOKENS
    new_factor = 0.2 * factor_slab + 0.8 * covariance
    block_rows = D // N_DP
    permuted = input_inverse.reshape(D, N_DP, block_rows)[:, owner_table, :].reshape(D, D)
    preconditioned = jnp.dot(permuted, gradient, preferred_element_type=jnp.float32)
    new_momentum = 0.9 * momentum + preconditioned
    return new_momentum, new_factor
```

```python
import functools

import jax
import jax.numpy as jnp
from jax import lax
from jax.experimental import pallas as pl
from jax.experimental.pallas import tpu as pltpu
from jax.sharding import PartitionSpec as P

MESH = pl.DeviceIdType.MESH
BF = jnp.bfloat16
F32 = jnp.float32
NX, NY, NL = 4, 4, 8
BR = 48
TK = 256
SLAB = 1536
CH = NL * BR
CG = 768
Z_ORDER = (1, 7, 2, 6, 3, 5, 4)


def kernel(
    at, gt, ainv, oinv, fac, mom, out_m, out_f,
    ra, rg, lhs, ai, oi, cvf, cs, cr, yp, yc, yhs, yhr, yb,
    pp, pys, pyr, pa, pls, plr, pq, pf, mf, ms, mr,
    loc, t0s, t0r, fws, fwr, zs, ys, lr, ais, air, ois, oir, cvs, cvr, yss, ysr,
    pyss, pysr, plss, plsr, pfzs, pfys, pfr, mss, msr,
):
    dp = lax.axis_index("dp")
    g = lax.axis_index("grad")
    x = lax.div(dp, 32)
    y = lax.rem(lax.div(dp, 8), 4)
    l = lax.rem(dp, 8)
    h = lax.div(g, 2)
    c = lax.rem(g, 2)

    def dev(x_=None, y_=None, l_=None, h_=None, c_=None):
        x_ = x if x_ is None else x_
        y_ = y if y_ is None else y_
        l_ = l if l_ is None else l_
        h_ = h if h_ is None else h_
        c_ = c if c_ is None else c_
        return ((x_ * NY + y_) * NL + l_, h_ * 2 + c_)

    def rows(i, n):
        return pl.ds(pl.multiple_of(i * n, 16), n)

    def lanes(i, n):
        return pl.ds(pl.multiple_of(i * n, 128), n)

    pending = []

    def send(src, dst, ss, rs, to):
        cp = pltpu.make_async_remote_copy(
            src_ref=src, dst_ref=dst, send_sem=ss, recv_sem=rs, device_id=to, device_id_type=MESH
        )
        cp.start()
        pending.append(cp)

    def arrived(dst, sem):
        pltpu.make_async_copy(dst, dst, sem).wait()

    xk = [lax.rem(x + k, NX) for k in range(NX)]
    yk = [lax.rem(y + k, NY) for k in range(NY)]
    lk = [lax.rem(l + k, NL) for k in range(NL)]

    own_o = pltpu.make_async_copy(oinv.at[:, lanes(g, CG)], oi.at[rows(x, BR)], loc.at[0])
    own_o.start()
    own_a = pltpu.make_async_copy(ainv, ai.at[rows(x, BR)], loc.at[1])
    own_a.start()

    bar = pltpu.get_barrier_semaphore()

    def greet(to):
        pl.semaphore_signal(bar, inc=1, device_id=to, device_id_type=MESH)

    greet(dev(c_=1 - c))
    greet(dev(h_=1 - h))
    for k in range(1, NL):
        greet(dev(l_=lk[k]))
    for k in range(1, NX):
        greet(dev(x_=xk[k]))
        greet(dev(y_=yk[k]))
    for j in range(2):
        x0 = c + 2 * j

        @pl.when(jnp.logical_or(x0 != x, x != g))
        def _():
            greet(dev(x_=x0, h_=lax.div(x, 2), c_=lax.rem(x, 2)))

    pl.semaphore_wait(bar, 17 - jnp.where(x == g, 1, 0))

    cc = lax.rem(x, 2)
    xj = lax.div(x, 2)
    t0 = []
    for a, (src, dst) in enumerate(((at, ra), (gt, rg))):
        near = pltpu.make_async_remote_copy(
            src_ref=src, dst_ref=dst.at[rows(x, BR)], send_sem=t0s.at[a, 0], recv_sem=t0r.at[a, xj],
            device_id=dev(x_=g, c_=cc), device_id_type=MESH,
        )
        far = pltpu.make_async_remote_copy(
            src_ref=src, dst_ref=dst.at[rows(x, BR)], send_sem=t0s.at[a, 1], recv_sem=t0r.at[a, xj],
            device_id=dev(x_=g, h_=1 - h, c_=cc), device_id_type=MESH,
        )
        here = pltpu.make_async_copy(src, dst.at[rows(x, BR)], t0r.at[a, xj])
        far.start()

        @pl.when(x != g)
        def _(near=near):
            near.start()

        @pl.when(x == g)
        def _(here=here):
            here.start()

        t0.append(near)
        pending.append(far)

    own_o.wait()
    for k in range(1, NX):
        r = rows(x, BR)
        send(oi.at[r], oi.at[r], ois.at[k - 1], oir.at[k - 1], dev(x_=xk[k]))
    own_a.wait()
    for k in range(1, NX):
        r = rows(x, BR)
        send(ai.at[r], ai.at[r], ais.at[k - 1], air.at[k - 1], dev(x_=xk[k]))

    def x_from(k):
        return lax.rem(x + (NX - k), NX)

    def y_from(k):
        return lax.rem(y + (NY - k), NY)

    def l_from(k):
        return lax.rem(l + (NL - k), NL)

    blk = ra.at[rows(g, BR)]
    mine = rows(y * NL + l, BR)
    arrived(blk, t0r.at[0, h])
    for k in Z_ORDER:
        send(blk, lhs.at[mine], zs.at[k - 1], lr.at[y * NL + l], dev(l_=lk[k]))
    for k in range(1, NY):
        send(blk, lhs.at[mine], ys.at[0, k - 1], lr.at[y * NL + l], dev(y_=yk[k]))
    lhs[mine, :] = ra[rows(g, BR), :]
    send(blk, blk, fws.at[0, 0], fwr.at[0, h], dev(c_=1 - c))
    other = ra.at[rows(c + 2 * (1 - h), BR)]
    arrived(other, t0r.at[0, 1 - h])
    send(other, other, fws.at[0, 1], fwr.at[0, 1 - h], dev(c_=1 - c))

    for j in range(2):
        b = rg.at[rows(c + 2 * j, BR)]
        arrived(b, t0r.at[1, j])
        send(b, b, fws.at[1, j], fwr.at[1, j], dev(c_=1 - c))
    for j in range(2):
        arrived(rg.at[rows(1 - c + 2 * j, BR)], fwr.at[1, j])
    for k in range(1, NX):
        arrived(oi.at[rows(x_from(k), BR)], oir.at[k - 1])
    gm = rg[...].astype(F32).T.astype(BF)
    part = jnp.dot(gm, oi[...], preferred_element_type=F32)
    pp[...] = part
    pys[...] = part.astype(BF)
    for k in range(1, NY):
        send(pys.at[rows(yk[k], 64)], pyr.at[k - 1], pyss.at[k - 1], pysr.at[k - 1], dev(y_=yk[k]))

    for k in Z_ORDER:
        i = y * NL + l_from(k)
        arrived(lhs.at[rows(i, BR)], lr.at[i])
        for q in range(1, NY):
            send(lhs.at[rows(i, BR)], lhs.at[rows(i, BR)], ys.at[k, q - 1], lr.at[i], dev(y_=yk[q]))

    for k in range(1, NY):
        arrived(pyr.at[k - 1], pysr.at[k - 1])
    acc = pp[rows(y, 64), :]
    for k in range(1, NY):
        acc = acc + pyr[k - 1].astype(F32)
    pa[...] = acc
    pls[...] = acc.astype(BF)

    def piece(l_):
        return rows(lax.div(l_, 2), 16), lanes(lax.rem(l_, 2), 384)

    for k in Z_ORDER:
        r, q = piece(lk[k])
        send(pls.at[r, q], plr.at[k - 1], plss.at[k - 1], plsr.at[k - 1], dev(l_=lk[k]))

    for j in range(2):
        arrived(ra.at[rows(1 - c + 2 * j, BR)], fwr.at[0, j])
    for k in range(1, NX):
        arrived(ai.at[rows(x_from(k), BR)], air.at[k - 1])

    def chunk(j, first):
        yy = y_from(j)
        f = lhs[rows(yy, CH), :]
        w = ai[:, lanes(yy, CH)]
        add = jnp.dot(w, f, preferred_element_type=F32)
        yp[...] = add if first else yp[...] + add
        cov = lax.dot_general(ra[...], f, (((1,), (1,)), ((), ())), preferred_element_type=F32)
        cvf[:, lanes(yy, CH)] = cov
        cs[:, lanes(yy, CH)] = cov.astype(BF)

    def chunk_send(j):
        yy = y_from(j)
        for k in range(1, NX):
            send(
                cs.at[rows(xk[k], BR), lanes(yy, CH)], cr.at[k - 1, :, lanes(yy, CH)],
                cvs.at[k - 1, j], cvr.at[k - 1, j], dev(x_=xk[k]),
            )

    chunk(0, True)
    chunk_send(0)

    for k in Z_ORDER:
        arrived(plr.at[k - 1], plsr.at[k - 1])
    r, q = piece(l)
    acc = pa[r, q]
    for k in range(1, NL):
        acc = acc + plr[k - 1].astype(F32)
    done = acc.astype(BF)
    pq[...] = done

    def place(y_, l_):
        return (
            pl.ds(pl.multiple_of(y_ * 64 + lax.div(l_, 2) * 16, 16), 16),
            lanes(lax.rem(l_, 2), 384),
        )

    r, q = place(y, l)
    pf[r, q] = done
    for k in Z_ORDER:
        send(pq, pf.at[r, q], pfzs.at[k - 1], pfr.at[y * NL + l], dev(l_=lk[k]))
    for k in range(1, NY):
        send(pq, pf.at[r, q], pfys.at[0, k - 1], pfr.at[y * NL + l], dev(y_=yk[k]))

    for j in range(1, NY):
        yy = y_from(j)
        for b in range(NL):
            arrived(lhs.at[rows(yy * NL + b, BR)], lr.at[yy * NL + b])
        chunk(j, False)
        if j == NY - 1:
            half = rows(1 - c, 96)
            send(yp.at[half], yc, yss.at[0], ysr.at[0], dev(c_=1 - c))
        chunk_send(j)

    for k in Z_ORDER:
        i = l_from(k)
        r, q = place(y, i)
        arrived(pf.at[r, q], pfr.at[y * NL + i])
        for n in range(1, NY):
            send(pf.at[r, q], pf.at[r, q], pfys.at[k, n - 1], pfr.at[y * NL + i], dev(y_=yk[n]))

    arrived(yc, ysr.at[0])
    keep = rows(c, 96)
    ysum = yp[keep, :] + yc[...]
    yhs[...] = ysum.astype(BF)
    send(yhs, yhr, yss.at[1], ysr.at[1], dev(h_=1 - h))

    for k in range(1, NX):
        for j in range(NY):
            s = lanes(y_from(j), CH)
            arrived(cr.at[k - 1, :, s], cvr.at[k - 1, j])
    cov = cvf[rows(x, BR), :]
    for k in range(1, NX):
        cov = cov + cr[k - 1].astype(F32)
    out_f[...] = 0.2 * fac[...] + 0.8 * (cov * (1.0 / 1024.0))

    arrived(yhr, ysr.at[1])
    yb[keep, :] = (ysum + yhr[...].astype(F32)).astype(BF)
    send(yb.at[keep], yb.at[keep], yss.at[2], ysr.at[2], dev(c_=1 - c))

    for j in range(1, NY):
        for b in range(NL):
            r, q = place(yk[j], b)
            arrived(pf.at[r, q], pfr.at[yk[j] * NL + b])
    arrived(yb.at[rows(1 - c, 96)], ysr.at[2])

    res = jnp.dot(yb[...], pf[...], preferred_element_type=F32)
    mf[...] = res
    ms[...] = res.astype(BF)
    for k in range(1, NX):
        send(ms.at[rows(xk[k], BR)], mr.at[k - 1], mss.at[k - 1], msr.at[k - 1], dev(x_=xk[k]))
    acc = mf[rows(x, BR), :]
    for k in range(1, NX):
        arrived(mr.at[k - 1], msr.at[k - 1])
        acc = acc + mr[k - 1].astype(F32)
    out_m[...] = 0.9 * mom[...] + acc

    for near in t0:

        @pl.when(x != g)
        def _(near=near):
            near.wait_send()

    for cp in pending:
        cp.wait_send()


def shards(
    activations, output_grads, output_inverse, input_inverse, owner_table, factor_slab, momentum
):
    g = lax.axis_index("grad")
    owners = lax.dynamic_slice(owner_table, (g * 32,), (32,))
    ainv = input_inverse.reshape(BR, 128, BR)[:, owners, :].reshape(BR, SLAB)
    vm = pl.BlockSpec(memory_space=pltpu.VMEM)
    dma = pltpu.SemaphoreType.DMA
    new_momentum, factor_t = pl.pallas_call(
        kernel,
        out_shape=(
            jax.ShapeDtypeStruct((BR, CG), F32),
            jax.ShapeDtypeStruct((BR, SLAB), F32),
        ),
        in_specs=[vm, vm, vm, pl.BlockSpec(memory_space=pl.ANY), vm, vm],
        out_specs=(vm, vm),
        scratch_shapes=[
            pltpu.VMEM((192, TK), BF),
            pltpu.VMEM((192, TK), BF),
            pltpu.VMEM((SLAB, TK), BF),
            pltpu.VMEM((192, SLAB), BF),
            pltpu.VMEM((192, CG), BF),
            pltpu.VMEM((192, SLAB), F32),
            pltpu.VMEM((192, SLAB), BF),
            pltpu.VMEM((3, BR, SLAB), BF),
            pltpu.VMEM((192, TK), F32),
            pltpu.VMEM((96, TK), F32),
            pltpu.VMEM((96, TK), BF),
            pltpu.VMEM((96, TK), BF),
            pltpu.VMEM((192, TK), BF),
            pltpu.VMEM((TK, CG), F32),
            pltpu.VMEM((TK, CG), BF),
            pltpu.VMEM((3, 64, CG), BF),
            pltpu.VMEM((64, CG), F32),
            pltpu.VMEM((64, CG), BF),
            pltpu.VMEM((7, 16, 384), BF),
            pltpu.VMEM((16, 384), BF),
            pltpu.VMEM((TK, CG), BF),
            pltpu.VMEM((192, CG), F32),
            pltpu.VMEM((192, CG), BF),
            pltpu.VMEM((3, BR, CG), BF),
            dma((2,)), dma((2, 2)), dma((2, 2)), dma((2, 2)), dma((2, 2)),
            dma((7,)), dma((8, 3)), dma((32,)),
            dma((3,)), dma((3,)), dma((3,)), dma((3,)),
            dma((3, 4)), dma((3, 4)), dma((3,)), dma((3,)),
            dma((3,)), dma((3,)), dma((7,)), dma((7,)),
            dma((7,)), dma((8, 3)), dma((32,)), dma((3,)), dma((3,)),
        ],
        compiler_params=pltpu.CompilerParams(
            collective_id=0, has_side_effects=True, vmem_limit_bytes=32 << 20
        ),
        cost_estimate=pl.CostEstimate(
            flops=2 * 230_000_000, bytes_accessed=2_000_000, transcendentals=0
        ),
        name="kfac",
    )(activations.T, output_grads.T, ainv, output_inverse, factor_slab.T, momentum)
    return (new_momentum, factor_t.T)


def solution(mesh):
    return jax.shard_map(
        shards,
        mesh=mesh,
        in_specs=(
            P("grad", "dp"),
            P("grad", "dp"),
            P("dp", None),
            P("dp", None),
            P(),
            P("grad", "dp"),
            P("dp", "grad"),
        ),
        out_specs=(P("dp", "grad"), P("grad", "dp")),
        check_vma=False,
    )
```

```python
import functools

import jax
import jax.numpy as jnp
from jax import lax
from jax.experimental import pallas as pl
from jax.experimental.pallas import tpu as pltpu
from jax.sharding import PartitionSpec as P

MESH = pl.DeviceIdType.MESH
BF = jnp.bfloat16
F32 = jnp.float32
NX, NY, NL = 4, 4, 8
BR = 48
TK = 256
SLAB = 1536
CH = NL * BR
CG = 768


def kernel(
    at, gt, ainv, oinv, owners, fac, mom, out_m, out_f,
    av, ow, fv, mv, ra, rg, lhs, an, ap, ai, oi, cvf, cs, cr, yp, yc, yhs, yhr, yb,
    pp, pys, pyr, pa, pls, plr, pb, pbs, plp, pq, pf, mf, ms, mr,
    loc, t0s, t0r, fws, fwr, zs, ys, lr, ais, air, ois, oir, cvs, cvr, yss, ysr,
    pyss, pysr, plss, plsr, pfzs, pfys, pfr, mss, msr,
):
    dp = lax.axis_index("dp")
    g = lax.axis_index("grad")
    x = lax.div(dp, 32)
    y = lax.rem(lax.div(dp, 8), 4)
    l = lax.rem(dp, 8)
    h = lax.div(g, 2)
    c = lax.rem(g, 2)

    def dev(x_=None, y_=None, l_=None, h_=None, c_=None):
        x_ = x if x_ is None else x_
        y_ = y if y_ is None else y_
        l_ = l if l_ is None else l_
        h_ = h if h_ is None else h_
        c_ = c if c_ is None else c_
        return ((x_ * NY + y_) * NL + l_, h_ * 2 + c_)

    def rows(i, n):
        return pl.ds(pl.multiple_of(i * n, 16), n)

    def lanes(i, n):
        return pl.ds(pl.multiple_of(i * n, 128), n)

    pending = []

    def send(src, dst, ss, rs, to):
        cp = pltpu.make_async_remote_copy(
            src_ref=src, dst_ref=dst, send_sem=ss, recv_sem=rs, device_id=to, device_id_type=MESH
        )
        cp.start()
        pending.append(cp)

    def arrived(dst, sem):
        pltpu.make_async_copy(dst, dst, sem).wait()

    xk = [lax.rem(x + k, NX) for k in range(NX)]
    yk = [lax.rem(y + k, NY) for k in range(NY)]
    quad = lax.div(l, 4)
    lp = lax.rem(l + 4, NL)
    lq = [quad * 4 + lax.rem(l + k, 4) for k in range(4)]

    def x_from(k):
        return lax.rem(x + (NX - k), NX)

    def y_from(k):
        return lax.rem(y + (NY - k), NY)

    def lq_from(k):
        return quad * 4 + lax.rem(l + (4 - k), 4)

    own = [
        pltpu.make_async_copy(owners, ow, loc.at[0]),
        pltpu.make_async_copy(ainv, av, loc.at[1]),
        pltpu.make_async_copy(oinv.at[:, lanes(g, CG)], oi.at[rows(x, BR)], loc.at[2]),
        pltpu.make_async_copy(mom, mv, loc.at[3]),
        pltpu.make_async_copy(fac, fv, loc.at[4]),
    ]
    for cp in own:
        cp.start()

    bar = pltpu.get_barrier_semaphore()

    def greet(to):
        pl.semaphore_signal(bar, inc=1, device_id=to, device_id_type=MESH)

    for j in range(2):
        x0 = c + 2 * j

        @pl.when(jnp.logical_or(x0 != x, x != g))
        def _():
            greet(dev(x_=x0, h_=lax.div(x, 2), c_=lax.rem(x, 2)))

    greet(dev(h_=1 - h))
    greet(dev(l_=lp))
    for k in range(1, NX):
        greet(dev(x_=xk[k]))
        greet(dev(y_=yk[k]))
        greet(dev(l_=lq[k]))
    greet(dev(c_=1 - c))

    own[1].wait()
    for j in range(16):
        an[pl.ds(j * CH, CH), 0:BR] = av[:, pl.ds(j * CH, CH)].astype(F32).T

    pl.semaphore_wait(bar, 14 - jnp.where(x == g, 1, 0))

    cc = lax.rem(x, 2)
    xj = lax.div(x, 2)

    def first(a, src, dst):
        there = pltpu.make_async_remote_copy(
            src_ref=src, dst_ref=dst.at[rows(x, BR)], send_sem=t0s.at[a, 0], recv_sem=t0r.at[a, xj],
            device_id=dev(x_=g, h_=xj, c_=cc), device_id_type=MESH,
        )
        here = pltpu.make_async_copy(src, dst.at[rows(x, BR)], t0r.at[a, xj])

        @pl.when(x != g)
        def _():
            there.start()

        @pl.when(x == g)
        def _():
            here.start()

        return there

    def second(a, src, dst):
        send(src, dst.at[rows(x, BR)], t0s.at[a, 1], t0r.at[a, xj], dev(x_=g, h_=1 - xj, c_=cc))

    t0 = [first(0, at, ra)]
    second(1, gt, rg)
    t0.append(first(1, gt, rg))
    r = rows(x, BR)
    own[2].wait()
    for k in range(1, NX):
        send(oi.at[r], oi.at[r], ois.at[k - 1], oir.at[k - 1], dev(x_=xk[k]))

    own[0].wait()
    natural = lax.broadcasted_iota(jnp.int32, (32, 128), 1)
    pick = jnp.where(ow[pl.ds(pl.multiple_of(g * 32, 8), 32), :] == natural, 1.0, 0.0).astype(BF)
    for j in range(BR):
        col = an[pl.ds(j, 128, stride=BR), :].astype(BF)
        ap[pl.ds(j, 32, stride=BR), :] = jnp.dot(pick, col, preferred_element_type=F32)

    blk = ra.at[rows(g, BR)]
    mine = rows(y * NL + l, BR)
    arrived(blk, t0r.at[0, h])
    send(blk, lhs.at[mine], zs.at[0], lr.at[y * NL + l], dev(l_=lp))
    for k in range(1, 4):
        send(blk, lhs.at[mine], zs.at[k], lr.at[y * NL + l], dev(l_=lq[k]))
    for k in range(1, NY):
        send(blk, lhs.at[mine], ys.at[0, k - 1], lr.at[y * NL + l], dev(y_=yk[k]))
    lhs[mine, :] = ra[rows(g, BR), :]
    send(blk, blk, fws.at[0, 0], fwr.at[0, h], dev(c_=1 - c))

    for j in range(2):
        b = rg.at[rows(c + 2 * j, BR)]
        arrived(b, t0r.at[1, j])
        send(b, b, fws.at[1, j], fwr.at[1, j], dev(c_=1 - c))
    for j in range(2):
        arrived(rg.at[rows(1 - c + 2 * j, BR)], fwr.at[1, j])
    for k in range(1, NX):
        arrived(oi.at[rows(x_from(k), BR)], oir.at[k - 1])
    gm = rg[...].astype(F32).T.astype(BF)
    part = jnp.dot(gm, oi[...], preferred_element_type=F32)
    pp[...] = part
    pys[...] = part.astype(BF)
    for k in range(1, NY):
        send(pys.at[rows(yk[k], 64)], pyr.at[k - 1], pyss.at[k - 1], pysr.at[k - 1], dev(y_=yk[k]))

    def to_y(i, n):
        s = lhs.at[rows(i, BR)]
        for q in range(1, NY):
            send(s, s, ys.at[n, q - 1], lr.at[i], dev(y_=yk[q]))

    i = y * NL + lp
    s = lhs.at[rows(i, BR)]
    arrived(s, lr.at[i])
    for k in range(1, 4):
        send(s, s, zs.at[3 + k], lr.at[i], dev(l_=lq[k]))
    to_y(i, 1)
    for k in (1, 3, 2):
        i = y * NL + lq_from(k)
        arrived(lhs.at[rows(i, BR)], lr.at[i])
        to_y(i, 1 + k)

    for j in range(NY):
        ai[r, pl.ds(j * CH, CH)] = ap[pl.ds(j * CH, CH), 0:BR].T.astype(BF)
    for k in range(1, NX):
        send(ai.at[r], ai.at[r], ais.at[k - 1], air.at[k - 1], dev(x_=xk[k]))
    second(0, at, ra)

    for k in range(1, NY):
        arrived(pyr.at[k - 1], pysr.at[k - 1])
    acc = pp[rows(y, 64), :]
    for k in range(1, NY):
        acc = acc + pyr[k - 1].astype(F32)
    pa[...] = acc
    pls[...] = acc.astype(BF)
    for k in (1, 3, 2):
        b = rows(lax.rem(lq[k], 4), 16)
        send(pls.at[b], plr.at[k - 1], plss.at[k - 1], plsr.at[k - 1], dev(l_=lq[k]))

    for k in (1, 3, 2):
        i = y * NL + lax.rem(lq_from(k) + 4, NL)
        arrived(lhs.at[rows(i, BR)], lr.at[i])
        to_y(i, 4 + k)

    for k in (1, 3, 2):
        arrived(plr.at[k - 1], plsr.at[k - 1])
    acc = pa[rows(lax.rem(l, 4), 16), :]
    for k in range(1, 4):
        acc = acc + plr[k - 1].astype(F32)
    pb[...] = acc
    pbs[...] = acc.astype(BF)
    send(pbs.at[:, lanes(1 - quad, 384)], plp, plss.at[3], plsr.at[3], dev(l_=lp))

    for k in range(1, NX):
        arrived(ai.at[rows(x_from(k), BR)], air.at[k - 1])

    def y_part(j):
        f = lhs[rows(y_from(j), CH), :]
        w = ai[:, lanes(y_from(j), CH)]
        add = jnp.dot(w, f, preferred_element_type=F32)
        yp[...] = add if j == 0 else yp[...] + add

    y_part(0)

    arrived(plp, plsr.at[3])
    done = (pb[:, lanes(quad, 384)] + plp[...].astype(F32)).astype(BF)
    pq[...] = done

    def place(y_, l_):
        return (
            pl.ds(pl.multiple_of(y_ * 64 + lax.rem(l_, 4) * 16, 16), 16),
            lanes(lax.div(l_, 4), 384),
        )

    r, q = place(y, l)
    pf[r, q] = done
    send(pq, pf.at[r, q], pfzs.at[0], pfr.at[y * NL + l], dev(l_=lp))
    for k in range(1, 4):
        send(pq, pf.at[r, q], pfzs.at[k], pfr.at[y * NL + l], dev(l_=lq[k]))
    for k in range(1, NY):
        send(pq, pf.at[r, q], pfys.at[0, k - 1], pfr.at[y * NL + l], dev(y_=yk[k]))

    for j in range(1, NY):
        yy = y_from(j)
        for b in range(NL):
            arrived(lhs.at[rows(yy * NL + b, BR)], lr.at[yy * NL + b])
        y_part(j)
    send(yp.at[rows(1 - c, 96)], yc, yss.at[0], ysr.at[0], dev(c_=1 - c))

    def pf_to_y(i, n):
        r, q = place(y, i)
        for m in range(1, NY):
            send(pf.at[r, q], pf.at[r, q], pfys.at[n, m - 1], pfr.at[y * NL + i], dev(y_=yk[m]))

    r, q = place(y, lp)
    arrived(pf.at[r, q], pfr.at[y * NL + lp])
    for k in range(1, 4):
        send(pf.at[r, q], pf.at[r, q], pfzs.at[3 + k], pfr.at[y * NL + lp], dev(l_=lq[k]))
    pf_to_y(lp, 1)

    arrived(yc, ysr.at[0])
    keep = rows(c, 96)
    ysum = yp[keep, :] + yc[...]
    yhs[...] = ysum.astype(BF)
    send(yhs, yhr, yss.at[1], ysr.at[1], dev(h_=1 - h))

    for k in (1, 3, 2):
        i = lq_from(k)
        r, q = place(y, i)
        arrived(pf.at[r, q], pfr.at[y * NL + i])
        pf_to_y(i, 1 + k)
    for k in (1, 3, 2):
        i = lax.rem(lq_from(k) + 4, NL)
        r, q = place(y, i)
        arrived(pf.at[r, q], pfr.at[y * NL + i])
        pf_to_y(i, 4 + k)

    other = ra.at[rows(c + 2 * (1 - h), BR)]
    arrived(other, t0r.at[0, 1 - h])
    send(other, other, fws.at[0, 1], fwr.at[0, 1 - h], dev(c_=1 - c))
    for j in range(2):
        arrived(ra.at[rows(1 - c + 2 * j, BR)], fwr.at[0, j])
    for j in range(NY):
        s = lanes(y_from(j), CH)
        f = lhs[rows(y_from(j), CH), :]
        cov = lax.dot_general(ra[...], f, (((1,), (1,)), ((), ())), preferred_element_type=F32)
        cvf[:, s] = cov
        cs[:, s] = cov.astype(BF)
        for k in range(1, NX):
            send(
                cs.at[rows(xk[k], BR), s], cr.at[k - 1, :, s],
                cvs.at[k - 1, j], cvr.at[k - 1, j], dev(x_=xk[k]),
            )

    arrived(yhr, ysr.at[1])
    yb[keep, :] = (ysum + yhr[...].astype(F32)).astype(BF)
    send(yb.at[keep], yb.at[keep], yss.at[2], ysr.at[2], dev(c_=1 - c))

    for j in range(1, NY):
        for b in range(NL):
            r, q = place(yk[j], b)
            arrived(pf.at[r, q], pfr.at[yk[j] * NL + b])
    arrived(yb.at[rows(1 - c, 96)], ysr.at[2])

    for k in range(1, NX):
        b = rows(xk[k], BR)
        ms[b, :] = jnp.dot(yb[b, :], pf[...], preferred_element_type=F32).astype(BF)
        send(ms.at[b], mr.at[k - 1], mss.at[k - 1], msr.at[k - 1], dev(x_=xk[k]))
    own[3].wait()
    mf[...] = 0.9 * mv[...] + jnp.dot(yb[rows(x, BR), :], pf[...], preferred_element_type=F32)

    for k in range(1, NX):
        for j in range(NY):
            s = lanes(y_from(j), CH)
            arrived(cr.at[k - 1, :, s], cvr.at[k - 1, j])
    own[4].wait()
    cov = cvf[rows(x, BR), :]
    for k in range(1, NX):
        cov = cov + cr[k - 1].astype(F32)
    out_f[...] = 0.2 * fv[...] + 0.8 * (cov * (1.0 / 1024.0))

    acc = mf[...]
    for k in range(1, NX):
        arrived(mr.at[k - 1], msr.at[k - 1])
        acc = acc + mr[k - 1].astype(F32)
    out_m[...] = acc

    for there in t0:

        @pl.when(x != g)
        def _(there=there):
            there.wait_send()

    for cp in pending:
        cp.wait_send()


def shards(
    activations, output_grads, output_inverse, input_inverse, owner_table, factor_slab, momentum
):
    vm = pl.BlockSpec(memory_space=pltpu.VMEM)
    dma = pltpu.SemaphoreType.DMA
    new_momentum, factor_t = pl.pallas_call(
        kernel,
        out_shape=(
            jax.ShapeDtypeStruct((BR, CG), F32),
            jax.ShapeDtypeStruct((BR, SLAB), F32),
        ),
        in_specs=[pl.BlockSpec(memory_space=pl.ANY)] * 7,
        out_specs=(vm, vm),
        scratch_shapes=[
            pltpu.VMEM((BR, 128 * BR), BF),
            pltpu.VMEM((128, 1), jnp.int32),
            pltpu.VMEM((BR, SLAB), F32),
            pltpu.VMEM((BR, CG), F32),
            pltpu.VMEM((192, TK), BF),
            pltpu.VMEM((192, TK), BF),
            pltpu.VMEM((SLAB, TK), BF),
            pltpu.VMEM((128 * BR, 128), F32),
            pltpu.VMEM((SLAB, 128), F32),
            pltpu.VMEM((192, SLAB), BF),
            pltpu.VMEM((192, CG), BF),
            pltpu.VMEM((192, SLAB), F32),
            pltpu.VMEM((192, SLAB), BF),
            pltpu.VMEM((3, BR, SLAB), BF),
            pltpu.VMEM((192, TK), F32),
            pltpu.VMEM((96, TK), F32),
            pltpu.VMEM((96, TK), BF),
            pltpu.VMEM((96, TK), BF),
            pltpu.VMEM((192, TK), BF),
            pltpu.VMEM((TK, CG), F32),
            pltpu.VMEM((TK, CG), BF),
            pltpu.VMEM((3, 64, CG), BF),
            pltpu.VMEM((64, CG), F32),
            pltpu.VMEM((64, CG), BF),
            pltpu.VMEM((3, 16, CG), BF),
            pltpu.VMEM((16, CG), F32),
            pltpu.VMEM((16, CG), BF),
            pltpu.VMEM((16, 384), BF),
            pltpu.VMEM((16, 384), BF),
            pltpu.VMEM((TK, CG), BF),
            pltpu.VMEM((BR, CG), F32),
            pltpu.VMEM((192, CG), BF),
            pltpu.VMEM((3, BR, CG), BF),
            dma((5,)), dma((2, 2)), dma((2, 2)), dma((2, 2)), dma((2, 2)),
            dma((7,)), dma((8, 3)), dma((32,)),
            dma((3,)), dma((3,)), dma((3,)), dma((3,)),
            dma((3, 4)), dma((3, 4)), dma((3,)), dma((3,)),
            dma((3,)), dma((3,)), dma((4,)), dma((4,)),
            dma((7,)), dma((8, 3)), dma((32,)), dma((3,)), dma((3,)),
        ],
        compiler_params=pltpu.CompilerParams(
            collective_id=0, has_side_effects=True, vmem_limit_bytes=56 << 20
        ),
        cost_estimate=pl.CostEstimate(
            flops=2 * 230_000_000, bytes_accessed=2_000_000, transcendentals=0
        ),
        name="kfac",
    )(
        activations.T, output_grads.T, input_inverse, output_inverse, owner_table[:, None], factor_slab.T, momentum
    )
    return (new_momentum, factor_t.T)


def solution(mesh):
    return jax.shard_map(
        shards,
        mesh=mesh,
        in_specs=(
            P("grad", "dp"),
            P("grad", "dp"),
            P("dp", None),
            P("dp", None),
            P(),
            P("grad", "dp"),
            P("dp", "grad"),
        ),
        out_specs=(P("dp", "grad"), P("grad", "dp")),
        check_vma=False,
    )
```

```python
import functools

import jax
import jax.numpy as jnp
from jax import lax
from jax.experimental import pallas as pl
from jax.experimental.pallas import tpu as pltpu
from jax.sharding import PartitionSpec as P

MESH = pl.DeviceIdType.MESH
BF = jnp.bfloat16
F32 = jnp.float32
NX, NY, NL = 4, 4, 8
BR = 48
TK = 256
SLAB = 1536
CH = NL * BR
CG = 768


def kernel(
    at, gt, ainv, oinv, owners, fac, mom, out_m, out_f,
    av, ow, fv, mv, ra, rg, lhs, an, ap, asb, ai, oi, cvf, cs, crc, cg, cfin, yp, ysb, yr, yb,
    pp, pys, pyr, pa, pls, plr, pb, pbs, plp, pq, pf, mo, mr, mf, ms, fin,
    loc, gs, gr, ars, arr, zs, ys, lr, ais, air, ois, oir, ccs, ccr, cfs, cfr,
    yss, ysr, yas, yar, pyss, pysr, plss, plsr, pfzs, pfys, pfr, mcs, mcr, mfs, mfr,
):
    dp = lax.axis_index("dp")
    g = lax.axis_index("grad")
    x = lax.div(dp, 32)
    y = lax.rem(lax.div(dp, 8), 4)
    l = lax.rem(dp, 8)
    h = lax.div(g, 2)
    c = lax.rem(g, 2)

    def dev(x_=None, y_=None, l_=None, h_=None, c_=None):
        x_ = x if x_ is None else x_
        y_ = y if y_ is None else y_
        l_ = l if l_ is None else l_
        h_ = h if h_ is None else h_
        c_ = c if c_ is None else c_
        return ((x_ * NY + y_) * NL + l_, h_ * 2 + c_)

    def rows(i, n):
        return pl.ds(pl.multiple_of(i * n, 16), n)

    def lanes(i, n):
        return pl.ds(pl.multiple_of(i * n, 128), n)

    pending = []

    def send(src, dst, ss, rs, to):
        cp = pltpu.make_async_remote_copy(
            src_ref=src, dst_ref=dst, send_sem=ss, recv_sem=rs, device_id=to, device_id_type=MESH
        )
        cp.start()
        pending.append(cp)

    def arrived(dst, sem):
        pltpu.make_async_copy(dst, dst, sem).wait()

    xk = [lax.rem(x + k, NX) for k in range(NX)]
    yk = [lax.rem(y + k, NY) for k in range(NY)]
    quad = lax.div(l, 4)
    lp = lax.rem(l + 4, NL)
    lq = [quad * 4 + lax.rem(l + k, 4) for k in range(4)]

    def x_from(k):
        return lax.rem(x + (NX - k), NX)

    def y_from(k):
        return lax.rem(y + (NY - k), NY)

    def lq_from(k):
        return quad * 4 + lax.rem(l + (4 - k), 4)

    mine = rows(y * NL + l, BR)
    r = rows(x, BR)
    own = [
        pltpu.make_async_copy(owners, ow, loc.at[0]),
        pltpu.make_async_copy(ainv, av, loc.at[1]),
        pltpu.make_async_copy(oinv.at[:, lanes(x, CG)], oi.at[r], loc.at[2]),
        pltpu.make_async_copy(gt, rg.at[r], loc.at[3]),
        pltpu.make_async_copy(at, ra.at[r], loc.at[4]),
        pltpu.make_async_copy(at, lhs.at[mine], loc.at[5]),
        pltpu.make_async_copy(mom, mv, loc.at[6]),
        pltpu.make_async_copy(fac, fv, loc.at[7]),
    ]
    for cp in own:
        cp.start()

    bar = pltpu.get_barrier_semaphore()

    def greet(to):
        pl.semaphore_signal(bar, inc=1, device_id=to, device_id_type=MESH)

    for j in range(2):

        @pl.when(jnp.logical_or(h != j, x != g))
        def _():
            greet(dev(x_=g, h_=j, c_=lax.rem(x, 2)))

    greet(dev(l_=lp))
    for k in range(1, NX):
        greet(dev(x_=xk[k]))
        greet(dev(y_=yk[k]))
        greet(dev(l_=lq[k]))
    greet(dev(c_=1 - c))

    own[1].wait()
    for j in range(16):
        an[pl.ds(j * CH, CH), 0:BR] = av[:, pl.ds(j * CH, CH)].astype(F32).T
    own[0].wait()

    pl.semaphore_wait(bar, 13 - jnp.where(x == g, 1, 0))

    send(at, lhs.at[mine], zs.at[0], lr.at[y * NL + l], dev(l_=lp))
    for k in range(1, NX):
        send(gt, rg.at[r], gs.at[k - 1], gr.at[k - 1], dev(x_=xk[k]))
    for k in range(1, 4):
        send(at, lhs.at[mine], zs.at[k], lr.at[y * NL + l], dev(l_=lq[k]))
    for k in range(1, NX):
        send(oinv.at[:, lanes(xk[k], CG)], oi.at[r], ois.at[k - 1], oir.at[k - 1], dev(x_=xk[k]))
    for k in range(1, NY):
        send(at, lhs.at[mine], ys.at[0, k - 1], lr.at[y * NL + l], dev(y_=yk[k]))

    natural = lax.broadcasted_iota(jnp.int32, (128, 128), 1)
    pick = jnp.where(ow[...] == natural, 1.0, 0.0).astype(BF)
    for j in range(BR):
        col = an[pl.ds(j, 128, stride=BR), :].astype(BF)
        ap[pl.ds(j, 128, stride=BR), :] = jnp.dot(pick, col, preferred_element_type=F32)

    def to_y(i, n):
        s = lhs.at[rows(i, BR)]
        for q in range(1, NY):
            send(s, s, ys.at[n, q - 1], lr.at[i], dev(y_=yk[q]))

    i = y * NL + lp
    s = lhs.at[rows(i, BR)]
    arrived(s, lr.at[i])
    for k in range(1, 4):
        send(s, s, zs.at[3 + k], lr.at[i], dev(l_=lq[k]))
    to_y(i, 1)
    own[2].wait()
    own[3].wait()
    for k in range(1, NX):
        arrived(rg.at[rows(x_from(k), BR)], gr.at[k - 1])
    for k in range(1, NX):
        arrived(oi.at[rows(x_from(k), BR)], oir.at[k - 1])
    gm = rg[...].astype(F32).T.astype(BF)
    part = jnp.dot(gm, oi[...], preferred_element_type=F32)
    pp[...] = part
    pys[...] = part.astype(BF)
    for k in range(1, NY):
        send(pys.at[rows(yk[k], 64)], pyr.at[k - 1], pyss.at[k - 1], pysr.at[k - 1], dev(y_=yk[k]))

    for k in (1, 3, 2):
        i = y * NL + lq_from(k)
        arrived(lhs.at[rows(i, BR)], lr.at[i])
        to_y(i, 1 + k)

    for j in range(16):
        asb[:, pl.ds(j * CH, CH)] = ap[pl.ds(j * CH, CH), 0:BR].T.astype(BF)
    for k in range(1, NX):
        send(asb.at[:, lanes(xk[k], SLAB)], ai.at[r], ais.at[k - 1], air.at[k - 1], dev(x_=xk[k]))
    keep = pltpu.make_async_copy(asb.at[:, lanes(x, SLAB)], ai.at[r], loc.at[8])
    keep.start()
    for k in range(1, NX):
        send(at, ra.at[r], ars.at[k - 1], arr.at[k - 1], dev(x_=xk[k]))

    for k in range(1, NY):
        arrived(pyr.at[k - 1], pysr.at[k - 1])
    acc = pp[rows(y, 64), :]
    for k in range(1, NY):
        acc = acc + pyr[k - 1].astype(F32)
    pa[...] = acc
    pls[...] = acc.astype(BF)
    for k in (1, 3, 2):
        b = rows(lax.rem(lq[k], 4), 16)
        send(pls.at[b], plr.at[k - 1], plss.at[k - 1], plsr.at[k - 1], dev(l_=lq[k]))

    for k in (1, 3, 2):
        i = y * NL + lax.rem(lq_from(k) + 4, NL)
        arrived(lhs.at[rows(i, BR)], lr.at[i])
        to_y(i, 4 + k)

    for k in (1, 3, 2):
        arrived(plr.at[k - 1], plsr.at[k - 1])
    acc = pa[rows(lax.rem(l, 4), 16), :]
    for k in range(1, 4):
        acc = acc + plr[k - 1].astype(F32)
    pb[...] = acc
    pbs[...] = acc.astype(BF)
    send(pbs.at[:, lanes(1 - quad, 384)], plp, plss.at[3], plsr.at[3], dev(l_=lp))

    own[5].wait()
    keep.wait()
    for k in range(1, NX):
        arrived(ai.at[rows(x_from(k), BR)], air.at[k - 1])

    def y_part(j):
        f = lhs[rows(y_from(j), CH), :]
        w = ai[:, lanes(y_from(j), CH)]
        add = jnp.dot(w, f, preferred_element_type=F32)
        yp[...] = add if j == 0 else yp[...] + add

    y_part(0)

    arrived(plp, plsr.at[3])
    done = (pb[:, lanes(quad, 384)] + plp[...].astype(F32)).astype(BF)
    pq[...] = done

    def place(y_, l_):
        return (
            pl.ds(pl.multiple_of(y_ * 64 + lax.rem(l_, 4) * 16, 16), 16),
            lanes(lax.div(l_, 4), 384),
        )

    r, q = place(y, l)
    pf[r, q] = done
    send(pq, pf.at[r, q], pfzs.at[0], pfr.at[y * NL + l], dev(l_=lp))
    for k in range(1, 4):
        send(pq, pf.at[r, q], pfzs.at[k], pfr.at[y * NL + l], dev(l_=lq[k]))
    for k in range(1, NY):
        send(pq, pf.at[r, q], pfys.at[0, k - 1], pfr.at[y * NL + l], dev(y_=yk[k]))

    for j in range(1, NY):
        yy = y_from(j)
        for b in range(NL):
            arrived(lhs.at[rows(yy * NL + b, BR)], lr.at[yy * NL + b])
        y_part(j)

    ysb[...] = yp[...].astype(BF)
    for k in range(1, NX):
        send(ysb.at[rows(xk[k], BR)], yr.at[k - 1], yss.at[k - 1], ysr.at[k - 1], dev(x_=xk[k]))

    def pf_to_y(i, n):
        r, q = place(y, i)
        for m in range(1, NY):
            send(pf.at[r, q], pf.at[r, q], pfys.at[n, m - 1], pfr.at[y * NL + i], dev(y_=yk[m]))

    r, q = place(y, lp)
    arrived(pf.at[r, q], pfr.at[y * NL + lp])
    for k in range(1, 4):
        send(pf.at[r, q], pf.at[r, q], pfzs.at[3 + k], pfr.at[y * NL + lp], dev(l_=lq[k]))
    pf_to_y(lp, 1)

    for k in range(1, NX):
        arrived(yr.at[k - 1], ysr.at[k - 1])
    acc = yp[rows(x, BR), :]
    for k in range(1, NX):
        acc = acc + yr[k - 1].astype(F32)
    r = rows(x, BR)
    yb[r, :] = acc.astype(BF)
    for k in range(1, NX):
        send(yb.at[r], yb.at[r], yas.at[k - 1], yar.at[k - 1], dev(x_=xk[k]))

    for k in (1, 3, 2):
        i = lq_from(k)
        r, q = place(y, i)
        arrived(pf.at[r, q], pfr.at[y * NL + i])
        pf_to_y(i, 1 + k)
    for k in (1, 3, 2):
        i = lax.rem(lq_from(k) + 4, NL)
        r, q = place(y, i)
        arrived(pf.at[r, q], pfr.at[y * NL + i])
        pf_to_y(i, 4 + k)

    own[4].wait()
    for k in range(1, NX):
        arrived(ra.at[rows(x_from(k), BR)], arr.at[k - 1])
    for j in range(NY):
        s = lanes(y_from(j), CH)
        f = lhs[rows(y_from(j), CH), :]
        cov = lax.dot_general(ra[...], f, (((1,), (1,)), ((), ())), preferred_element_type=F32)
        cvf[:, s] = cov
        cs[:, s] = cov.astype(BF)
        for b in range(2):
            send(
                cs.at[rows(1 - c + 2 * b, BR), s], crc.at[b, :, s],
                ccs.at[b, j], ccr.at[b, j], dev(c_=1 - c),
            )

    parted = []

    def to_owner(src, dst, ss, rs, b):
        there = pltpu.make_async_remote_copy(
            src_ref=src, dst_ref=dst, send_sem=ss, recv_sem=rs,
            device_id=dev(x_=c + 2 * b, h_=lax.div(x, 2), c_=lax.rem(x, 2)), device_id_type=MESH,
        )
        here = pltpu.make_async_copy(src, dst, rs)
        is_own = jnp.logical_and(x == g, h == b)

        @pl.when(jnp.logical_not(is_own))
        def _():
            there.start()

        @pl.when(is_own)
        def _():
            here.start()

        parted.append((there, is_own))

    def cov_to_owner():
        for j in range(NY):
            s = lanes(y_from(j), CH)
            for b in range(2):
                arrived(crc.at[b, :, s], ccr.at[b, j])
                cg[b, :, s] = (cvf[rows(c + 2 * b, BR), s] + crc[b, :, s].astype(F32)).astype(BF)
                to_owner(cg.at[b, :, s], cfin.at[h, :, s], cfs.at[b, j], cfr.at[h, j], b)

    cov_to_owner()

    for j in range(1, NY):
        for b in range(NL):
            r, q = place(yk[j], b)
            arrived(pf.at[r, q], pfr.at[yk[j] * NL + b])
    for k in range(1, NX):
        arrived(yb.at[rows(x_from(k), BR)], yar.at[k - 1])

    for b in range(2):
        mo[b] = jnp.dot(yb[rows(1 - c + 2 * b, BR), :], pf[...], preferred_element_type=F32)
        send(mo.at[b], mr.at[b], mcs.at[b], mcr.at[b], dev(c_=1 - c))
    for b in range(2):
        mf[b] = jnp.dot(yb[rows(c + 2 * b, BR), :], pf[...], preferred_element_type=F32)
    for b in range(2):
        arrived(mr.at[b], mcr.at[b])
        ms[b] = (mf[b] + mr[b]).astype(BF)
        to_owner(ms.at[b], fin.at[h], mfs.at[b], mfr.at[h], b)

    own[7].wait()
    for k in range(2):
        for j in range(NY):
            s = lanes(y_from(j), CH)
            arrived(cfin.at[k, :, s], cfr.at[k, j])
    cov = cfin[0].astype(F32) + cfin[1].astype(F32)
    out_f[...] = 0.2 * fv[...] + 0.8 * (cov * (1.0 / 1024.0))

    own[6].wait()
    for k in range(2):
        arrived(fin.at[k], mfr.at[k])
    out_m[...] = 0.9 * mv[...] + (fin[0].astype(F32) + fin[1].astype(F32))

    for there, is_own in parted:

        @pl.when(jnp.logical_not(is_own))
        def _(there=there):
            there.wait_send()

    for cp in pending:
        cp.wait_send()


def shards(
    activations, output_grads, output_inverse, input_inverse, owner_table, factor_slab, momentum
):
    vm = pl.BlockSpec(memory_space=pltpu.VMEM)
    dma = pltpu.SemaphoreType.DMA
    new_momentum, factor_t = pl.pallas_call(
        kernel,
        out_shape=(
            jax.ShapeDtypeStruct((BR, CG), F32),
            jax.ShapeDtypeStruct((BR, SLAB), F32),
        ),
        in_specs=[pl.BlockSpec(memory_space=pl.ANY)] * 7,
        out_specs=(vm, vm),
        scratch_shapes=[
            pltpu.VMEM((BR, 128 * BR), BF),
            pltpu.VMEM((128, 1), jnp.int32),
            pltpu.VMEM((BR, SLAB), F32),
            pltpu.VMEM((BR, CG), F32),
            pltpu.VMEM((192, TK), BF),
            pltpu.VMEM((192, TK), BF),
            pltpu.VMEM((SLAB, TK), BF),
            pltpu.VMEM((128 * BR, 128), F32),
            pltpu.VMEM((128 * BR, 128), F32),
            pltpu.VMEM((BR, 128 * BR), BF),
            pltpu.VMEM((192, SLAB), BF),
            pltpu.VMEM((192, CG), BF),
            pltpu.VMEM((192, SLAB), F32),
            pltpu.VMEM((192, SLAB), BF),
            pltpu.VMEM((2, BR, SLAB), BF),
            pltpu.VMEM((2, BR, SLAB), BF),
            pltpu.VMEM((2, BR, SLAB), BF),
            pltpu.VMEM((192, TK), F32),
            pltpu.VMEM((192, TK), BF),
            pltpu.VMEM((3, BR, TK), BF),
            pltpu.VMEM((192, TK), BF),
            pltpu.VMEM((TK, CG), F32),
            pltpu.VMEM((TK, CG), BF),
            pltpu.VMEM((3, 64, CG), BF),
            pltpu.VMEM((64, CG), F32),
            pltpu.VMEM((64, CG), BF),
            pltpu.VMEM((3, 16, CG), BF),
            pltpu.VMEM((16, CG), F32),
            pltpu.VMEM((16, CG), BF),
            pltpu.VMEM((16, 384), BF),
            pltpu.VMEM((16, 384), BF),
            pltpu.VMEM((TK, CG), BF),
            pltpu.VMEM((2, BR, CG), F32),
            pltpu.VMEM((2, BR, CG), F32),
            pltpu.VMEM((2, BR, CG), F32),
            pltpu.VMEM((2, BR, CG), BF),
            pltpu.VMEM((2, BR, CG), BF),
            dma((9,)),
            dma((3,)),
            dma((3,)),
            dma((3,)),
            dma((3,)),
            dma((7,)),
            dma((8, 3)),
            dma((32,)),
            dma((3,)),
            dma((3,)),
            dma((3,)),
            dma((3,)),
            dma((2, 4)),
            dma((2, 4)),
            dma((2, 4)),
            dma((2, 4)),
            dma((3,)),
            dma((3,)),
            dma((3,)),
            dma((3,)),
            dma((3,)),
            dma((3,)),
            dma((4,)),
            dma((4,)),
            dma((7,)),
            dma((8, 3)),
            dma((32,)),
            dma((2,)),
            dma((2,)),
            dma((2,)),
            dma((2,)),
        ],
        compiler_params=pltpu.CompilerParams(
            collective_id=0, has_side_effects=True, vmem_limit_bytes=56 << 20
        ),
        cost_estimate=pl.CostEstimate(
            flops=2 * 230_000_000, bytes_accessed=2_000_000, transcendentals=0
        ),
        name="kfac",
    )(
        activations.T, output_grads.T, input_inverse, output_inverse, owner_table[:, None], factor_slab.T, momentum
    )
    return (new_momentum, factor_t.T)


def solution(mesh):
    return jax.shard_map(
        shards,
        mesh=mesh,
        in_specs=(
            P("grad", "dp"),
            P("grad", "dp"),
            P("dp", None),
            P("dp", None),
            P(),
            P("grad", "dp"),
            P("dp", "grad"),
        ),
        out_specs=(P("dp", "grad"), P("grad", "dp")),
        check_vma=False,
    )
```

```python
import functools

import jax
import jax.numpy as jnp
from jax import lax
from jax.experimental import pallas as pl
from jax.experimental.pallas import tpu as pltpu
from jax.sharding import PartitionSpec as P

MESH = pl.DeviceIdType.MESH
BF = jnp.bfloat16
F32 = jnp.float32
NX, NY, NL = 4, 4, 8
BR = 48
TK = 256
SLAB = 1536
CH = NL * BR
CG = 768


def kernel(
    at, gt, ainv, oinv, owners, fac, mom, out_m, out_f,
    av, ow, pk, fv, mv, ra, rg, lhs, an, ap, ai, oi, cvf, cs, cr, yp, yc, yhs, yhr, yb,
    pg, pp, pys, pyr, pa, pls, plr, pb, pbs, plp, pq, pf, mf, ms, mr,
    loc, t0s, t0r, fws, fwr, zs, ys, lr, ais, air, ois, oir, cvs, cvr, yss, ysr,
    pyss, pysr, plss, plsr, pfzs, pfys, pfr, mss, msr,
):
    dp = lax.axis_index("dp")
    g = lax.axis_index("grad")
    x = lax.div(dp, 32)
    y = lax.rem(lax.div(dp, 8), 4)
    l = lax.rem(dp, 8)
    h = lax.div(g, 2)
    c = lax.rem(g, 2)

    def dev(x_=None, y_=None, l_=None, h_=None, c_=None):
        x_ = x if x_ is None else x_
        y_ = y if y_ is None else y_
        l_ = l if l_ is None else l_
        h_ = h if h_ is None else h_
        c_ = c if c_ is None else c_
        return ((x_ * NY + y_) * NL + l_, h_ * 2 + c_)

    def rows(i, n):
        return pl.ds(pl.multiple_of(i * n, 16), n)

    def lanes(i, n):
        return pl.ds(pl.multiple_of(i * n, 128), n)

    pending = []

    def send(src, dst, ss, rs, to):
        cp = pltpu.make_async_remote_copy(
            src_ref=src, dst_ref=dst, send_sem=ss, recv_sem=rs, device_id=to, device_id_type=MESH
        )
        cp.start()
        pending.append(cp)

    def arrived(dst, sem):
        pltpu.make_async_copy(dst, dst, sem).wait()

    xk = [lax.rem(x + k, NX) for k in range(NX)]
    yk = [lax.rem(y + k, NY) for k in range(NY)]
    quad = lax.div(l, 4)
    lp = lax.rem(l + 4, NL)
    lq = [quad * 4 + lax.rem(l + k, 4) for k in range(4)]

    def x_from(k):
        return lax.rem(x + (NX - k), NX)

    def y_from(k):
        return lax.rem(y + (NY - k), NY)

    def lq_from(k):
        return quad * 4 + lax.rem(l + (4 - k), 4)

    own = [
        pltpu.make_async_copy(owners, ow, loc.at[0]),
        pltpu.make_async_copy(ainv, av, loc.at[1]),
        pltpu.make_async_copy(oinv.at[:, lanes(g, CG)], oi.at[rows(x, BR)], loc.at[2]),
        pltpu.make_async_copy(mom, mv, loc.at[3]),
        pltpu.make_async_copy(fac, fv, loc.at[4]),
    ]
    for cp in own:
        cp.start()

    bar = pltpu.get_barrier_semaphore()

    def greet(to):
        pl.semaphore_signal(bar, inc=1, device_id=to, device_id_type=MESH)

    for j in range(2):
        x0 = c + 2 * j

        @pl.when(jnp.logical_or(x0 != x, x != g))
        def _():
            greet(dev(x_=x0, h_=lax.div(x, 2), c_=lax.rem(x, 2)))

    greet(dev(h_=1 - h))
    greet(dev(l_=lp))
    for k in range(1, NX):
        greet(dev(x_=xk[k]))
        greet(dev(y_=yk[k]))
        greet(dev(l_=lq[k]))
    greet(dev(c_=1 - c))

    own[1].wait()
    for j in range(16):
        an[pl.ds(j * CH, CH), 0:BR] = av[:, pl.ds(j * CH, CH)].astype(F32).T

    pl.semaphore_wait(bar, 14 - jnp.where(x == g, 1, 0))

    cc = lax.rem(x, 2)
    xj = lax.div(x, 2)

    def first(a, src, dst):
        there = pltpu.make_async_remote_copy(
            src_ref=src, dst_ref=dst.at[rows(x, BR)], send_sem=t0s.at[a, 0], recv_sem=t0r.at[a, xj],
            device_id=dev(x_=g, h_=xj, c_=cc), device_id_type=MESH,
        )
        here = pltpu.make_async_copy(src, dst.at[rows(x, BR)], t0r.at[a, xj])

        @pl.when(x != g)
        def _():
            there.start()

        @pl.when(x == g)
        def _():
            here.start()

        return there

    def second(a, src, dst):
        send(src, dst.at[rows(x, BR)], t0s.at[a, 1], t0r.at[a, xj], dev(x_=g, h_=1 - xj, c_=cc))

    t0 = [first(0, at, ra)]
    second(1, gt, rg)
    t0.append(first(1, gt, rg))
    r = rows(x, BR)
    own[2].wait()
    for k in range(1, NX):
        send(oi.at[r], oi.at[r], ois.at[k - 1], oir.at[k - 1], dev(x_=xk[k]))

    own[0].wait()
    natural = lax.broadcasted_iota(jnp.int32, (128, 128), 0)
    pk[...] = jnp.where(ow[...] == natural, 1.0, 0.0).T
    pick = pk[pl.ds(pl.multiple_of(g * 32, 8), 32), :].astype(BF)
    for j in range(BR):
        col = an[pl.ds(j, 128, stride=BR), :].astype(BF)
        ap[pl.ds(j, 32, stride=BR), :] = jnp.dot(pick, col, preferred_element_type=F32)

    blk = ra.at[rows(g, BR)]
    mine = rows(y * NL + l, BR)
    arrived(blk, t0r.at[0, h])
    send(blk, lhs.at[mine], zs.at[0], lr.at[y * NL + l], dev(l_=lp))
    for k in range(1, 4):
        send(blk, lhs.at[mine], zs.at[k], lr.at[y * NL + l], dev(l_=lq[k]))
    for k in range(1, NY):
        send(blk, lhs.at[mine], ys.at[0, k - 1], lr.at[y * NL + l], dev(y_=yk[k]))
    lhs[mine, :] = ra[rows(g, BR), :]
    send(blk, blk, fws.at[0, 0], fwr.at[0, h], dev(c_=1 - c))

    for j in range(2):
        b = rg.at[rows(c + 2 * j, BR)]
        arrived(b, t0r.at[1, j])
        send(b, b, fws.at[1, j], fwr.at[1, j], dev(c_=1 - c))
    for j in range(2):
        arrived(rg.at[rows(1 - c + 2 * j, BR)], fwr.at[1, j])
    for k in range(1, NX):
        arrived(oi.at[rows(x_from(k), BR)], oir.at[k - 1])
    gm = rg[...].astype(F32).T.astype(BF)
    pg[...] = gm
    for k in range(1, NY):
        b = rows(yk[k], 64)
        pys[b, :] = jnp.dot(pg[b, :], oi[...], preferred_element_type=F32).astype(BF)
        send(pys.at[rows(yk[k], 64)], pyr.at[k - 1], pyss.at[k - 1], pysr.at[k - 1], dev(y_=yk[k]))

    pp[...] = jnp.dot(pg[rows(y, 64), :], oi[...], preferred_element_type=F32)

    def to_y(i, n):
        s = lhs.at[rows(i, BR)]
        for q in range(1, NY):
            send(s, s, ys.at[n, q - 1], lr.at[i], dev(y_=yk[q]))

    i = y * NL + lp
    s = lhs.at[rows(i, BR)]
    arrived(s, lr.at[i])
    for k in range(1, 4):
        send(s, s, zs.at[3 + k], lr.at[i], dev(l_=lq[k]))
    to_y(i, 1)
    for k in (1, 3, 2):
        i = y * NL + lq_from(k)
        arrived(lhs.at[rows(i, BR)], lr.at[i])
        to_y(i, 1 + k)

    for j in range(NY):
        ai[r, pl.ds(j * CH, CH)] = ap[pl.ds(j * CH, CH), 0:BR].T.astype(BF)
    for k in range(1, NX):
        send(ai.at[r], ai.at[r], ais.at[k - 1], air.at[k - 1], dev(x_=xk[k]))
    second(0, at, ra)

    for k in range(1, NY):
        arrived(pyr.at[k - 1], pysr.at[k - 1])
    acc = pp[...]
    for k in range(1, NY):
        acc = acc + pyr[k - 1].astype(F32)
    pa[...] = acc
    pls[...] = acc.astype(BF)
    for k in (1, 3, 2):
        b = rows(lax.rem(lq[k], 4), 16)
        send(pls.at[b], plr.at[k - 1], plss.at[k - 1], plsr.at[k - 1], dev(l_=lq[k]))

    for k in (1, 3, 2):
        i = y * NL + lax.rem(lq_from(k) + 4, NL)
        arrived(lhs.at[rows(i, BR)], lr.at[i])
        to_y(i, 4 + k)

    for k in (1, 3, 2):
        arrived(plr.at[k - 1], plsr.at[k - 1])
    acc = pa[rows(lax.rem(l, 4), 16), :]
    for k in range(1, 4):
        acc = acc + plr[k - 1].astype(F32)
    pb[...] = acc
    pbs[...] = acc.astype(BF)
    send(pbs.at[:, lanes(1 - quad, 384)], plp, plss.at[3], plsr.at[3], dev(l_=lp))

    for k in range(1, NX):
        arrived(ai.at[rows(x_from(k), BR)], air.at[k - 1])

    def y_part(j):
        f = lhs[rows(y_from(j), CH), :]
        w = ai[:, lanes(y_from(j), CH)]
        add = jnp.dot(w, f, preferred_element_type=F32)
        yp[...] = add if j == 0 else yp[...] + add

    y_part(0)

    arrived(plp, plsr.at[3])
    done = (pb[:, lanes(quad, 384)] + plp[...].astype(F32)).astype(BF)
    pq[...] = done

    def place(y_, l_):
        return (
            pl.ds(pl.multiple_of(y_ * 64 + lax.rem(l_, 4) * 16, 16), 16),
            lanes(lax.div(l_, 4), 384),
        )

    r, q = place(y, l)
    pf[r, q] = done
    send(pq, pf.at[r, q], pfzs.at[0], pfr.at[y * NL + l], dev(l_=lp))
    for k in range(1, 4):
        send(pq, pf.at[r, q], pfzs.at[k], pfr.at[y * NL + l], dev(l_=lq[k]))
    for k in range(1, NY):
        send(pq, pf.at[r, q], pfys.at[0, k - 1], pfr.at[y * NL + l], dev(y_=yk[k]))

    for j in range(1, NY):
        yy = y_from(j)
        for b in range(NL):
            arrived(lhs.at[rows(yy * NL + b, BR)], lr.at[yy * NL + b])
        y_part(j)
    send(yp.at[rows(1 - c, 96)], yc, yss.at[0], ysr.at[0], dev(c_=1 - c))

    def pf_to_y(i, n):
        r, q = place(y, i)
        for m in range(1, NY):
            send(pf.at[r, q], pf.at[r, q], pfys.at[n, m - 1], pfr.at[y * NL + i], dev(y_=yk[m]))

    r, q = place(y, lp)
    arrived(pf.at[r, q], pfr.at[y * NL + lp])
    for k in range(1, 4):
        send(pf.at[r, q], pf.at[r, q], pfzs.at[3 + k], pfr.at[y * NL + lp], dev(l_=lq[k]))
    pf_to_y(lp, 1)

    arrived(yc, ysr.at[0])
    keep = rows(c, 96)
    ysum = yp[keep, :] + yc[...]
    yhs[...] = ysum.astype(BF)
    send(yhs, yhr, yss.at[1], ysr.at[1], dev(h_=1 - h))

    for k in (1, 3, 2):
        i = lq_from(k)
        r, q = place(y, i)
        arrived(pf.at[r, q], pfr.at[y * NL + i])
        pf_to_y(i, 1 + k)
    for k in (1, 3, 2):
        i = lax.rem(lq_from(k) + 4, NL)
        r, q = place(y, i)
        arrived(pf.at[r, q], pfr.at[y * NL + i])
        pf_to_y(i, 4 + k)

    other = ra.at[rows(c + 2 * (1 - h), BR)]
    arrived(other, t0r.at[0, 1 - h])
    send(other, other, fws.at[0, 1], fwr.at[0, 1 - h], dev(c_=1 - c))
    for j in range(2):
        arrived(ra.at[rows(1 - c + 2 * j, BR)], fwr.at[0, j])
    for j in range(NY):
        s = lanes(y_from(j), CH)
        f = lhs[rows(y_from(j), CH), :]
        cov = lax.dot_general(ra[...], f, (((1,), (1,)), ((), ())), preferred_element_type=F32)
        cvf[:, s] = cov
        cs[:, s] = cov.astype(BF)
        for k in range(1, NX):
            send(
                cs.at[rows(xk[k], BR), s], cr.at[k - 1, :, s],
                cvs.at[k - 1, j], cvr.at[k - 1, j], dev(x_=xk[k]),
            )

    arrived(yhr, ysr.at[1])
    yb[keep, :] = (ysum + yhr[...].astype(F32)).astype(BF)
    send(yb.at[keep], yb.at[keep], yss.at[2], ysr.at[2], dev(c_=1 - c))

    for j in range(1, NY):
        for b in range(NL):
            r, q = place(yk[j], b)
            arrived(pf.at[r, q], pfr.at[yk[j] * NL + b])
    arrived(yb.at[rows(1 - c, 96)], ysr.at[2])

    for k in range(1, NX):
        b = rows(xk[k], BR)
        ms[b, :] = jnp.dot(yb[b, :], pf[...], preferred_element_type=F32).astype(BF)
        send(ms.at[b], mr.at[k - 1], mss.at[k - 1], msr.at[k - 1], dev(x_=xk[k]))
    own[3].wait()
    mf[...] = 0.9 * mv[...] + jnp.dot(yb[rows(x, BR), :], pf[...], preferred_element_type=F32)

    for k in range(1, NX):
        for j in range(NY):
            s = lanes(y_from(j), CH)
            arrived(cr.at[k - 1, :, s], cvr.at[k - 1, j])
    own[4].wait()
    cov = cvf[rows(x, BR), :]
    for k in range(1, NX):
        cov = cov + cr[k - 1].astype(F32)
    out_f[...] = 0.2 * fv[...] + 0.8 * (cov * (1.0 / 1024.0))

    acc = mf[...]
    for k in range(1, NX):
        arrived(mr.at[k - 1], msr.at[k - 1])
        acc = acc + mr[k - 1].astype(F32)
    out_m[...] = acc

    for there in t0:

        @pl.when(x != g)
        def _(there=there):
            there.wait_send()

    for cp in pending:
        cp.wait_send()


def shards(
    activations, output_grads, output_inverse, input_inverse, owner_table, factor_slab, momentum
):
    vm = pl.BlockSpec(memory_space=pltpu.VMEM)
    dma = pltpu.SemaphoreType.DMA
    new_momentum, factor_t = pl.pallas_call(
        kernel,
        out_shape=(
            jax.ShapeDtypeStruct((BR, CG), F32),
            jax.ShapeDtypeStruct((BR, SLAB), F32),
        ),
        in_specs=[pl.BlockSpec(memory_space=pl.ANY)] * 7,
        out_specs=(vm, vm),
        scratch_shapes=[
            pltpu.VMEM((BR, 128 * BR), BF),
            pltpu.VMEM((1, 128), jnp.int32),
            pltpu.VMEM((128, 128), F32),
            pltpu.VMEM((BR, SLAB), F32),
            pltpu.VMEM((BR, CG), F32),
            pltpu.VMEM((192, TK), BF),
            pltpu.VMEM((192, TK), BF),
            pltpu.VMEM((SLAB, TK), BF),
            pltpu.VMEM((128 * BR, 128), F32),
            pltpu.VMEM((SLAB, 128), F32),
            pltpu.VMEM((192, SLAB), BF),
            pltpu.VMEM((192, CG), BF),
            pltpu.VMEM((192, SLAB), F32),
            pltpu.VMEM((192, SLAB), BF),
            pltpu.VMEM((3, BR, SLAB), BF),
            pltpu.VMEM((192, TK), F32),
            pltpu.VMEM((96, TK), F32),
            pltpu.VMEM((96, TK), BF),
            pltpu.VMEM((96, TK), BF),
            pltpu.VMEM((192, TK), BF),
            pltpu.VMEM((TK, 192), BF),
            pltpu.VMEM((64, CG), F32),
            pltpu.VMEM((TK, CG), BF),
            pltpu.VMEM((3, 64, CG), BF),
            pltpu.VMEM((64, CG), F32),
            pltpu.VMEM((64, CG), BF),
            pltpu.VMEM((3, 16, CG), BF),
            pltpu.VMEM((16, CG), F32),
            pltpu.VMEM((16, CG), BF),
            pltpu.VMEM((16, 384), BF),
            pltpu.VMEM((16, 384), BF),
            pltpu.VMEM((TK, CG), BF),
            pltpu.VMEM((BR, CG), F32),
            pltpu.VMEM((192, CG), BF),
            pltpu.VMEM((3, BR, CG), BF),
            dma((5,)), dma((2, 2)), dma((2, 2)), dma((2, 2)), dma((2, 2)),
            dma((7,)), dma((8, 3)), dma((32,)),
            dma((3,)), dma((3,)), dma((3,)), dma((3,)),
            dma((3, 4)), dma((3, 4)), dma((3,)), dma((3,)),
            dma((3,)), dma((3,)), dma((4,)), dma((4,)),
            dma((7,)), dma((8, 3)), dma((32,)), dma((3,)), dma((3,)),
        ],
        compiler_params=pltpu.CompilerParams(
            collective_id=0, has_side_effects=True, vmem_limit_bytes=56 << 20
        ),
        cost_estimate=pl.CostEstimate(
            flops=2 * 230_000_000, bytes_accessed=2_000_000, transcendentals=0
        ),
        name="kfac",
    )(
        activations.T, output_grads.T, input_inverse, output_inverse, owner_table[None, :], factor_slab.T, momentum
    )
    return (new_momentum, factor_t.T)


def solution(mesh):
    return jax.shard_map(
        shards,
        mesh=mesh,
        in_specs=(
            P("grad", "dp"),
            P("grad", "dp"),
            P("dp", None),
            P("dp", None),
            P(),
            P("grad", "dp"),
            P("dp", "grad"),
        ),
        out_specs=(P("dp", "grad"), P("grad", "dp")),
        check_vma=False,
    )
```

```python
import functools

import jax
import jax.numpy as jnp
from jax import lax
from jax.experimental import pallas as pl
from jax.experimental.pallas import tpu as pltpu
from jax.sharding import PartitionSpec as P

MESH = pl.DeviceIdType.MESH
BF = jnp.bfloat16
F32 = jnp.float32
NX, NY, NL = 4, 4, 8
BR = 48
TK = 256
SLAB = 1536
CH = NL * BR
CG = 768


def kernel(
    at, gt, ainv, oinv, owners, fac, mom, out_m, out_f,
    av, ow, pk, fv, mv, ra, rg, lhs, an, ap, ai, oi, cvf, cs, cr, yp, yc, yhs, yhr, yb,
    pg, pp, pys, pyr, pa, pls, plr, pb, pbs, plp, pq, pf, mf, ms, mr,
    loc, t0s, t0r, fws, fwr, zs, ys, lr, ais, air, ois, oir, cvs, cvr, yss, ysr,
    pyss, pysr, plss, plsr, pfzs, pfys, pfr, mss, msr,
):
    dp = lax.axis_index("dp")
    g = lax.axis_index("grad")
    x = lax.div(dp, 32)
    y = lax.rem(lax.div(dp, 8), 4)
    l = lax.rem(dp, 8)
    h = lax.div(g, 2)
    c = lax.rem(g, 2)

    def dev(x_=None, y_=None, l_=None, h_=None, c_=None):
        x_ = x if x_ is None else x_
        y_ = y if y_ is None else y_
        l_ = l if l_ is None else l_
        h_ = h if h_ is None else h_
        c_ = c if c_ is None else c_
        return ((x_ * NY + y_) * NL + l_, h_ * 2 + c_)

    def rows(i, n):
        return pl.ds(pl.multiple_of(i * n, 16), n)

    def lanes(i, n):
        return pl.ds(pl.multiple_of(i * n, 128), n)

    pending = []

    def send(src, dst, ss, rs, to):
        cp = pltpu.make_async_remote_copy(
            src_ref=src, dst_ref=dst, send_sem=ss, recv_sem=rs, device_id=to, device_id_type=MESH
        )
        cp.start()
        pending.append(cp)

    def arrived(dst, sem):
        pltpu.make_async_copy(dst, dst, sem).wait()

    xk = [lax.rem(x + k, NX) for k in range(NX)]
    yk = [lax.rem(y + k, NY) for k in range(NY)]
    quad = lax.div(l, 4)
    lp = lax.rem(l + 4, NL)
    lq = [quad * 4 + lax.rem(l + k, 4) for k in range(4)]

    def x_from(k):
        return lax.rem(x + (NX - k), NX)

    def y_from(k):
        return lax.rem(y + (NY - k), NY)

    def lq_from(k):
        return quad * 4 + lax.rem(l + (4 - k), 4)

    own = [
        pltpu.make_async_copy(owners, ow, loc.at[0]),
        pltpu.make_async_copy(ainv, av, loc.at[1]),
        pltpu.make_async_copy(oinv.at[:, lanes(g, CG)], oi.at[rows(x, BR)], loc.at[2]),
        pltpu.make_async_copy(mom, mv, loc.at[3]),
        pltpu.make_async_copy(fac, fv, loc.at[4]),
    ]
    for cp in own:
        cp.start()

    bar = pltpu.get_barrier_semaphore()

    def greet(to):
        pl.semaphore_signal(bar, inc=1, device_id=to, device_id_type=MESH)

    for j in range(2):
        x0 = c + 2 * j

        @pl.when(jnp.logical_or(x0 != x, x != g))
        def _():
            greet(dev(x_=x0, h_=lax.div(x, 2), c_=lax.rem(x, 2)))

    greet(dev(h_=1 - h))
    greet(dev(l_=lp))
    for k in range(1, NX):
        greet(dev(x_=xk[k]))
        greet(dev(y_=yk[k]))
        greet(dev(l_=lq[k]))
    greet(dev(c_=1 - c))

    own[1].wait()
    for j in range(16):
        an[pl.ds(j * CH, CH), 0:BR] = av[:, pl.ds(j * CH, CH)].astype(F32).T

    pl.semaphore_wait(bar, 14 - jnp.where(x == g, 1, 0))

    cc = lax.rem(x, 2)
    xj = lax.div(x, 2)

    def first(a, src, dst):
        there = pltpu.make_async_remote_copy(
            src_ref=src, dst_ref=dst.at[rows(x, BR)], send_sem=t0s.at[a, 0], recv_sem=t0r.at[a, xj],
            device_id=dev(x_=g, h_=xj, c_=cc), device_id_type=MESH,
        )
        here = pltpu.make_async_copy(src, dst.at[rows(x, BR)], t0r.at[a, xj])

        @pl.when(x != g)
        def _():
            there.start()

        @pl.when(x == g)
        def _():
            here.start()

        return there

    def second(a, src, dst):
        send(src, dst.at[rows(x, BR)], t0s.at[a, 1], t0r.at[a, xj], dev(x_=g, h_=1 - xj, c_=cc))

    t0 = [first(0, at, ra)]
    second(1, gt, rg)
    t0.append(first(1, gt, rg))
    r = rows(x, BR)
    own[2].wait()
    for k in range(1, NX):
        send(oi.at[r], oi.at[r], ois.at[k - 1], oir.at[k - 1], dev(x_=xk[k]))

    own[0].wait()
    natural = lax.broadcasted_iota(jnp.int32, (128, 128), 0)
    pk[...] = jnp.where(ow[...] == natural, 1.0, 0.0).T
    pick = pk[pl.ds(pl.multiple_of(g * 32, 8), 32), :].astype(BF)
    for j in range(BR):
        col = an[pl.ds(j, 128, stride=BR), :].astype(BF)
        ap[pl.ds(j, 32, stride=BR), :] = jnp.dot(pick, col, preferred_element_type=F32)

    blk = ra.at[rows(g, BR)]
    mine = rows(y * NL + l, BR)
    arrived(blk, t0r.at[0, h])
    send(blk, lhs.at[mine], zs.at[0], lr.at[y * NL + l], dev(l_=lp))
    for k in range(1, 4):
        send(blk, lhs.at[mine], zs.at[k], lr.at[y * NL + l], dev(l_=lq[k]))
    for k in range(1, NY):
        send(blk, lhs.at[mine], ys.at[0, k - 1], lr.at[y * NL + l], dev(y_=yk[k]))
    lhs[mine, :] = ra[rows(g, BR), :]
    send(blk, blk, fws.at[0, 0], fwr.at[0, h], dev(c_=1 - c))

    for j in range(2):
        b = rg.at[rows(c + 2 * j, BR)]
        arrived(b, t0r.at[1, j])
        send(b, b, fws.at[1, j], fwr.at[1, j], dev(c_=1 - c))
    for j in range(2):
        arrived(rg.at[rows(1 - c + 2 * j, BR)], fwr.at[1, j])
    for k in range(1, NX):
        arrived(oi.at[rows(x_from(k), BR)], oir.at[k - 1])
    gm = rg[...].astype(F32).T.astype(BF)
    pg[...] = gm
    for k in range(1, NY):
        b = rows(yk[k], 64)
        pys[b, :] = jnp.dot(pg[b, :], oi[...], preferred_element_type=F32).astype(BF)
        send(pys.at[rows(yk[k], 64)], pyr.at[k - 1], pyss.at[k - 1], pysr.at[k - 1], dev(y_=yk[k]))

    pp[...] = jnp.dot(pg[rows(y, 64), :], oi[...], preferred_element_type=F32)

    def to_y(i, n):
        s = lhs.at[rows(i, BR)]
        for q in range(1, NY):
            send(s, s, ys.at[n, q - 1], lr.at[i], dev(y_=yk[q]))

    i = y * NL + lp
    s = lhs.at[rows(i, BR)]
    arrived(s, lr.at[i])
    for k in range(1, 4):
        send(s, s, zs.at[3 + k], lr.at[i], dev(l_=lq[k]))
    to_y(i, 1)
    for k in (1, 3, 2):
        i = y * NL + lq_from(k)
        arrived(lhs.at[rows(i, BR)], lr.at[i])
        to_y(i, 1 + k)

    for j in range(NY):
        ai[r, pl.ds(j * CH, CH)] = ap[pl.ds(j * CH, CH), 0:BR].T.astype(BF)
    for k in range(1, NX):
        send(ai.at[r], ai.at[r], ais.at[k - 1], air.at[k - 1], dev(x_=xk[k]))
    second(0, at, ra)

    for k in range(1, NY):
        arrived(pyr.at[k - 1], pysr.at[k - 1])
    acc = pp[...]
    for k in range(1, NY):
        acc = acc + pyr[k - 1].astype(F32)
    pa[...] = acc
    pls[...] = acc.astype(BF)
    for k in (1, 3, 2):
        b = rows(lax.rem(lq[k], 4), 16)
        send(pls.at[b], plr.at[k - 1], plss.at[k - 1], plsr.at[k - 1], dev(l_=lq[k]))

    for k in (1, 3, 2):
        i = y * NL + lax.rem(lq_from(k) + 4, NL)
        arrived(lhs.at[rows(i, BR)], lr.at[i])
        to_y(i, 4 + k)

    for k in (1, 3, 2):
        arrived(plr.at[k - 1], plsr.at[k - 1])
    acc = pa[rows(lax.rem(l, 4), 16), :]
    for k in range(1, 4):
        acc = acc + plr[k - 1].astype(F32)
    pb[...] = acc
    pbs[...] = acc.astype(BF)
    send(pbs.at[:, lanes(1 - quad, 384)], plp, plss.at[3], plsr.at[3], dev(l_=lp))

    for k in range(1, NX):
        arrived(ai.at[rows(x_from(k), BR)], air.at[k - 1])

    def y_part(j):
        f = lhs[rows(y_from(j), CH), :]
        w = ai[:, lanes(y_from(j), CH)]
        add = jnp.dot(w, f, preferred_element_type=F32)
        yp[...] = add if j == 0 else yp[...] + add

    y_part(0)

    arrived(plp, plsr.at[3])
    done = (pb[:, lanes(quad, 384)] + plp[...].astype(F32)).astype(BF)
    pq[...] = done

    def place(y_, l_):
        return (
            pl.ds(pl.multiple_of(y_ * 64 + lax.rem(l_, 4) * 16, 16), 16),
            lanes(lax.div(l_, 4), 384),
        )

    r, q = place(y, l)
    pf[r, q] = done
    send(pq, pf.at[r, q], pfzs.at[0], pfr.at[y * NL + l], dev(l_=lp))
    for k in range(1, 4):
        send(pq, pf.at[r, q], pfzs.at[k], pfr.at[y * NL + l], dev(l_=lq[k]))
    for k in range(1, NY):
        send(pq, pf.at[r, q], pfys.at[0, k - 1], pfr.at[y * NL + l], dev(y_=yk[k]))

    other = ra.at[rows(c + 2 * (1 - h), BR)]
    arrived(other, t0r.at[0, 1 - h])
    send(other, other, fws.at[0, 1], fwr.at[0, 1 - h], dev(c_=1 - c))
    for j in range(2):
        arrived(ra.at[rows(1 - c + 2 * j, BR)], fwr.at[0, j])
    def cov_part(j):
        s = lanes(y_from(j), CH)
        f = lhs[rows(y_from(j), CH), :]
        cov = lax.dot_general(ra[...], f, (((1,), (1,)), ((), ())), preferred_element_type=F32)
        cvf[:, s] = cov
        cs[:, s] = cov.astype(BF)
        for k in range(1, NX):
            send(
                cs.at[rows(xk[k], BR), s], cr.at[k - 1, :, s],
                cvs.at[k - 1, j], cvr.at[k - 1, j], dev(x_=xk[k]),
            )

    cov_part(0)
    for j in range(1, NY):
        yy = y_from(j)
        for b in range(NL):
            arrived(lhs.at[rows(yy * NL + b, BR)], lr.at[yy * NL + b])
        y_part(j)
        if j < NY - 1:
            cov_part(j)
    send(yp.at[rows(1 - c, 96)], yc, yss.at[0], ysr.at[0], dev(c_=1 - c))

    def pf_to_y(i, n):
        r, q = place(y, i)
        for m in range(1, NY):
            send(pf.at[r, q], pf.at[r, q], pfys.at[n, m - 1], pfr.at[y * NL + i], dev(y_=yk[m]))

    r, q = place(y, lp)
    arrived(pf.at[r, q], pfr.at[y * NL + lp])
    for k in range(1, 4):
        send(pf.at[r, q], pf.at[r, q], pfzs.at[3 + k], pfr.at[y * NL + lp], dev(l_=lq[k]))
    pf_to_y(lp, 1)

    arrived(yc, ysr.at[0])
    keep = rows(c, 96)
    ysum = yp[keep, :] + yc[...]
    yhs[...] = ysum.astype(BF)
    send(yhs, yhr, yss.at[1], ysr.at[1], dev(h_=1 - h))

    cov_part(NY - 1)

    for k in (1, 3, 2):
        i = lq_from(k)
        r, q = place(y, i)
        arrived(pf.at[r, q], pfr.at[y * NL + i])
        pf_to_y(i, 1 + k)
    for k in (1, 3, 2):
        i = lax.rem(lq_from(k) + 4, NL)
        r, q = place(y, i)
        arrived(pf.at[r, q], pfr.at[y * NL + i])
        pf_to_y(i, 4 + k)

    arrived(yhr, ysr.at[1])
    yb[keep, :] = (ysum + yhr[...].astype(F32)).astype(BF)
    send(yb.at[keep], yb.at[keep], yss.at[2], ysr.at[2], dev(c_=1 - c))

    for j in range(1, NY):
        for b in range(NL):
            r, q = place(yk[j], b)
            arrived(pf.at[r, q], pfr.at[yk[j] * NL + b])
    arrived(yb.at[rows(1 - c, 96)], ysr.at[2])

    for k in range(1, NX):
        b = rows(xk[k], BR)
        ms[b, :] = jnp.dot(yb[b, :], pf[...], preferred_element_type=F32).astype(BF)
        send(ms.at[b], mr.at[k - 1], mss.at[k - 1], msr.at[k - 1], dev(x_=xk[k]))
    own[3].wait()
    mf[...] = 0.9 * mv[...] + jnp.dot(yb[rows(x, BR), :], pf[...], preferred_element_type=F32)

    for k in range(1, NX):
        for j in range(NY):
            s = lanes(y_from(j), CH)
            arrived(cr.at[k - 1, :, s], cvr.at[k - 1, j])
    own[4].wait()
    cov = cvf[rows(x, BR), :]
    for k in range(1, NX):
        cov = cov + cr[k - 1].astype(F32)
    out_f[...] = 0.2 * fv[...] + 0.8 * (cov * (1.0 / 1024.0))

    acc = mf[...]
    for k in range(1, NX):
        arrived(mr.at[k - 1], msr.at[k - 1])
        acc = acc + mr[k - 1].astype(F32)
    out_m[...] = acc

    for there in t0:

        @pl.when(x != g)
        def _(there=there):
            there.wait_send()

    for cp in pending:
        cp.wait_send()


def shards(
    activations, output_grads, output_inverse, input_inverse, owner_table, factor_slab, momentum
):
    vm = pl.BlockSpec(memory_space=pltpu.VMEM)
    dma = pltpu.SemaphoreType.DMA
    new_momentum, factor_t = pl.pallas_call(
        kernel,
        out_shape=(
            jax.ShapeDtypeStruct((BR, CG), F32),
            jax.ShapeDtypeStruct((BR, SLAB), F32),
        ),
        in_specs=[pl.BlockSpec(memory_space=pl.ANY)] * 7,
        out_specs=(vm, vm),
        scratch_shapes=[
            pltpu.VMEM((BR, 128 * BR), BF),
            pltpu.VMEM((1, 128), jnp.int32),
            pltpu.VMEM((128, 128), F32),
            pltpu.VMEM((BR, SLAB), F32),
            pltpu.VMEM((BR, CG), F32),
            pltpu.VMEM((192, TK), BF),
            pltpu.VMEM((192, TK), BF),
            pltpu.VMEM((SLAB, TK), BF),
            pltpu.VMEM((128 * BR, 128), F32),
            pltpu.VMEM((SLAB, 128), F32),
            pltpu.VMEM((192, SLAB), BF),
            pltpu.VMEM((192, CG), BF),
            pltpu.VMEM((192, SLAB), F32),
            pltpu.VMEM((192, SLAB), BF),
            pltpu.VMEM((3, BR, SLAB), BF),
            pltpu.VMEM((192, TK), F32),
            pltpu.VMEM((96, TK), F32),
            pltpu.VMEM((96, TK), BF),
            pltpu.VMEM((96, TK), BF),
            pltpu.VMEM((192, TK), BF),
            pltpu.VMEM((TK, 192), BF),
            pltpu.VMEM((64, CG), F32),
            pltpu.VMEM((TK, CG), BF),
            pltpu.VMEM((3, 64, CG), BF),
            pltpu.VMEM((64, CG), F32),
            pltpu.VMEM((64, CG), BF),
            pltpu.VMEM((3, 16, CG), BF),
            pltpu.VMEM((16, CG), F32),
            pltpu.VMEM((16, CG), BF),
            pltpu.VMEM((16, 384), BF),
            pltpu.VMEM((16, 384), BF),
            pltpu.VMEM((TK, CG), BF),
            pltpu.VMEM((BR, CG), F32),
            pltpu.VMEM((192, CG), BF),
            pltpu.VMEM((3, BR, CG), BF),
            dma((5,)), dma((2, 2)), dma((2, 2)), dma((2, 2)), dma((2, 2)),
            dma((7,)), dma((8, 3)), dma((32,)),
            dma((3,)), dma((3,)), dma((3,)), dma((3,)),
            dma((3, 4)), dma((3, 4)), dma((3,)), dma((3,)),
            dma((3,)), dma((3,)), dma((4,)), dma((4,)),
            dma((7,)), dma((8, 3)), dma((32,)), dma((3,)), dma((3,)),
        ],
        compiler_params=pltpu.CompilerParams(
            collective_id=0, has_side_effects=True, vmem_limit_bytes=56 << 20
        ),
        cost_estimate=pl.CostEstimate(
            flops=2 * 230_000_000, bytes_accessed=2_000_000, transcendentals=0
        ),
        name="kfac",
    )(
        activations.T, output_grads.T, input_inverse, output_inverse, owner_table[None, :], factor_slab.T, momentum
    )
    return (new_momentum, factor_t.T)


def solution(mesh):
    return jax.shard_map(
        shards,
        mesh=mesh,
        in_specs=(
            P("grad", "dp"),
            P("grad", "dp"),
            P("dp", None),
            P("dp", None),
            P(),
            P("grad", "dp"),
            P("dp", "grad"),
        ),
        out_specs=(P("dp", "grad"), P("grad", "dp")),
        check_vma=False,
    )
```
